256 devices in a mesh: row: 16 (over x, z_lo, core), col: 16 (over z_hi, y).
Axes of the slice: x: 4, y: 4, z: 8 (z_hi: 4, z_lo: 2; z = z_hi * 2 + z_lo), core: 2. Of those that a mesh axis runs over, the one named last changes fastest.
Arguments:
- features: bfloat16 [131072, 256], P(('row', 'col')), may hold values from -6 to 6
- cotangent: bfloat16 [131072, 256], P(('row', 'col')), may hold values from -6 to 6
- w_self: bfloat16 [256, 256], replicated, may hold values from -0.375 to 0.375
- w_neigh: bfloat16 [256, 256], replicated, may hold values from -0.375 to 0.375
- bias_term: bfloat16 [256], replicated, may hold values from -3 to 3
- block_tiles: bfloat16 [16, 16, 256, 128, 128], P('row', 'col'), may hold values from 0 to 1
- block_rows: int32 [16, 16, 256], P('row', 'col'), may hold values from 0 to 63, as said below
- block_cols: int32 [16, 16, 256], P('row', 'col'), may hold values from 0 to 63
- block_counts: int32 [16, 16], P('row', 'col'), may hold values from 51 to 256, as said below
Outputs:
- activation: bfloat16 [131072, 256], P(('row', 'col'))
- grad_features: bfloat16 [131072, 256], P(('row', 'col'))
- grad_self: float32 [256, 256], replicated
- grad_neigh: float32 [256, 256], replicated
- grad_bias: float32 [256], replicated
The draws below stay inside these ranges and needn't reach their ends.
Inputs may be any that keep to these rules, and one draw needn't show every extreme that they name: `block_counts`: at least one device holds 256 live slots. `block_rows`: on each device the 256 slots name distinct (block row, block column) pairs; slots at or after the device's count are padding and carry no edges.
All inputs are finite; a program needn't handle non-finite values.
Results may differ from the reference program's by a relative error of at most 0.019.
Values may be sent and summed in bfloat16 or wider, within the bound.
No kernel may reach another device: no remote copies, remote signals or barrier semaphores. Data moves between devices by JAX's collectives and lax.ppermute only.
A program may use at most 128 MiB of HBM per device.

```python
import jax
import jax.numpy as jnp
from jax import lax

F = 256
BLK = 128
NODE_DEV = 512
MAXB = 256
NODES = 131072
DST_BLOCKS = 64
SRC_BLOCKS = 64
N_ROW = 16
N_COL = 16


def pair_table(key):
    keys = jax.random.split(key, N_ROW * N_COL)
    chosen = jax.vmap(lambda one_key: jax.random.permutation(one_key, DST_BLOCKS * SRC_BLOCKS)[:MAXB])(keys)
    return chosen.reshape(N_ROW, N_COL, MAXB).astype(jnp.int32)


def draw_block_rows(key, part):
    pairs = pair_table(key)
    return (pairs // SRC_BLOCKS).astype(jnp.int32)


def draw_block_cols(key, part):
    pairs = pair_table(key)
    return (pairs % SRC_BLOCKS).astype(jnp.int32)


def draw_block_counts(key, part):
    key = jax.random.fold_in(key, 5)
    base_key, hot_key, row_key, col_key = jax.random.split(key, 4)
    base = jax.random.randint(base_key, (N_ROW, N_COL), MAXB // 5, MAXB // 2 + 1)
    heavy = jax.random.randint(hot_key, (N_ROW, N_COL), 0, 6) == 0
    hot_row = jax.random.randint(row_key, (), 0, N_ROW)
    hot_col = jax.random.randint(col_key, (), 0, N_COL)
    marked = (jnp.arange(N_ROW)[:, None] == hot_row) & (jnp.arange(N_COL)[None, :] == hot_col)
    return jnp.where(heavy | marked, MAXB, base).astype(jnp.int32)


def level_of(stream_key, shape, cuts, least, high):
    def one(position, shards_of):
        draws = jax.random.uniform(jax.random.fold_in(jax.random.fold_in(stream_key, 6), position), (shards_of,), jnp.float32, least / len(cuts), high / len(cuts))
        return jnp.repeat(jnp.exp(draws), shape[position] // shards_of).reshape((-1,) + (1,) * (len(shape) - position - 1))

    level = one(*cuts[0])
    for cut in cuts[1:]:
        level = level * one(*cut)
    return level


def scatter_about(rng, extent, scale, most, cuts=(), kind=jnp.bfloat16):
    factor_of = level_of(rng, extent, cuts, -0.22, 0.18) if cuts else 1.0
    values = jax.random.normal(rng, extent, jnp.float32) * scale * factor_of
    return jnp.minimum(jnp.maximum(values, -most), most).astype(kind)


def setup_inputs(seed: int = 0) -> dict:
    key_of = jax.random.split(jax.random.key(seed), 10)
    return {
        "features": scatter_about(key_of[0], (NODES, F), 1.0, 6.0, ((0, 256),)),
        "cotangent": scatter_about(key_of[1], (NODES, F), 1.0, 6.0, ((0, 256),)),
        "w_self": scatter_about(key_of[2], (F, F), F ** -0.5, 0.375),
        "w_neigh": scatter_about(key_of[3], (F, F), F ** -0.5, 0.375),
        "bias_term": scatter_about(key_of[4], (F,), 0.5, 3.0),
        "block_tiles": jnp.clip(1.0 * jax.random.uniform(key_of[5], (N_ROW, N_COL, MAXB, BLK, BLK), jnp.float32) ** level_of(key_of[5], (N_ROW, N_COL, MAXB, BLK, BLK), ((0, 16), (1, 16)), -0.2, 0.2), 0.0, 1.0).astype(jnp.bfloat16),
        "block_rows": draw_block_rows(jax.random.fold_in(key_of[9], 71), 0),
        "block_cols": draw_block_cols(jax.random.fold_in(key_of[9], 71), 0),
        "block_counts": draw_block_counts(jax.random.fold_in(key_of[9], 71), 0),
    }


def reference(features, cotangent, w_self, w_neigh, bias_term, block_tiles, block_rows, block_cols, block_counts):
    pieces = features.reshape(N_ROW, N_COL, NODE_DEV, F)
    live_mask = (jnp.arange(MAXB)[None, None, :] < block_counts[:, :, None]).astype(jnp.float32)

    def forward_row(row_index):

        def one_device(carried, col_index):
            panel = pieces[:, col_index].reshape(SRC_BLOCKS, BLK, F).astype(jnp.float32)
            tiles_now = block_tiles[row_index, col_index].astype(jnp.float32) * live_mask[row_index, col_index][:, None, None]
            source = panel[block_cols[row_index, col_index]]
            contrib = jnp.einsum('bij,bjf->bif', tiles_now, source)
            targets = block_rows[row_index, col_index]
            summed = carried[0] + jax.ops.segment_sum(contrib, targets, DST_BLOCKS)
            degrees = carried[1] + jax.ops.segment_sum(lax.optimization_barrier(jnp.sum(tiles_now, axis=2)), targets, DST_BLOCKS)
            return ((summed, degrees), None)
        initial = (jnp.zeros((DST_BLOCKS, BLK, F), jnp.float32), jnp.zeros((DST_BLOCKS, BLK), jnp.float32))
        result, unused = lax.scan(one_device, initial, jnp.arange(N_COL))
        return result
    aggregate, degree = lax.map(forward_row, jnp.arange(N_ROW))
    aggregate = aggregate.reshape(NODES, F)
    scale = 1.0 / jnp.sqrt(1.0 + degree.reshape(NODES))
    neigh = (scale[:, None] * aggregate).astype(jnp.bfloat16)
    pre = jnp.dot(features, w_self, preferred_element_type=jnp.float32) + jnp.dot(neigh, w_neigh, preferred_element_type=jnp.float32) + bias_term.astype(jnp.float32)
    sigma = jax.nn.sigmoid(pre)
    activation = (pre * sigma).astype(jnp.bfloat16)
    dpre = (cotangent.astype(jnp.float32) * sigma * (1.0 + pre * (1.0 - sigma))).astype(jnp.bfloat16)
    norm_factor = 1.0 / jnp.sqrt(jnp.float32(NODES))
    grad_self = jnp.dot(features.T, dpre, preferred_element_type=jnp.float32) * norm_factor
    grad_neigh = jnp.dot(neigh.T, dpre, preferred_element_type=jnp.float32) * norm_factor
    grad_bias = lax.optimization_barrier(jnp.sum(dpre.astype(jnp.float32), axis=0)) * norm_factor
    back = (scale[:, None] * jnp.dot(dpre, w_neigh.T, preferred_element_type=jnp.float32)).astype(jnp.bfloat16)
    back_rows = back.reshape(N_ROW, DST_BLOCKS, BLK, F)

    def backward_col(col_index):

        def one_device(carried, row_index):
            tiles_now = block_tiles[row_index, col_index].astype(jnp.float32) * live_mask[row_index, col_index][:, None, None]
            source = back_rows[row_index][block_rows[row_index, col_index]].astype(jnp.float32)
            contrib = jnp.einsum('bji,bjf->bif', tiles_now, source)
            return (carried + jax.ops.segment_sum(contrib, block_cols[row_index, col_index], SRC_BLOCKS), None)
        initial = jnp.zeros((SRC_BLOCKS, BLK, F), jnp.float32)
        result, unused = lax.scan(one_device, initial, jnp.arange(N_ROW))
        return result
    partial_sums = lax.map(backward_col, jnp.arange(N_COL))
    transposed = partial_sums.reshape(N_COL, N_ROW, NODE_DEV, F).transpose(1, 0, 2, 3).reshape(NODES, F)
    grad_features = (jnp.dot(dpre, w_self.T, preferred_element_type=jnp.float32) + transposed).astype(jnp.bfloat16)
    return (activation, grad_features, grad_self, grad_neigh, grad_bias)
```

```python
import functools

import jax
import jax.numpy as jnp
from jax import lax
from jax.experimental import pallas as pl
from jax.experimental.pallas import tpu as pltpu
from jax.sharding import PartitionSpec as P

f32, bf16 = jnp.float32, jnp.bfloat16
BLK, F, SLOTS, BLOCKS = 128, 256, 256, 64
CHUNK = 512
PARTS = 8
UNROLL = 16

GRIDS = {
    "x": ("row", 4, 4),
    "zl": ("row", 2, 2),
    "core": ("row", 2, 1),
    "zh": ("col", 4, 4),
    "y": ("col", 4, 1),
}
RING_PLACE = (0, 2, 3, 1)
PLANE_PLACE = (0, 1, 3, 5, 4, 7, 2, 6)


def coordinate(axis):
    name, size, stride = GRIDS[axis]
    return lax.axis_index(name) // stride % size


def shift(value, axis, step):
    name, size, stride = GRIDS[axis]
    pairs = []
    for source in range(16):
        at = source // stride % size
        pairs.append((source, source + ((at + step) % size - at) * stride))
    return lax.ppermute(value, name, pairs)


def total(*terms):
    out = terms[0].astype(f32)
    for term in terms[1:]:
        out = out + term.astype(f32)
    return out


def added(*terms):
    return total(*terms).astype(bf16)


def look_up(table, index):
    out = jnp.zeros_like(index)
    for place, entry in enumerate(table):
        out = jnp.where(index == place, entry, out)
    return out


def gather_row(own):
    half = own.shape[0] // 2
    z0 = shift(own, "zl", 1)
    p1 = shift(own, "x", 1)
    m1 = shift(own, "x", -1)
    p2 = shift(p1, "x", 1)
    mz = shift(z0, "x", -1)
    pz = shift(p1, "zl", 1)
    top = shift(pz[:half], "x", 1)
    low = shift(mz[half:], "x", -1)
    mine = [own, z0, p1, m1, p2, mz, pz, top, low]
    return mine + [shift(piece, "core", 1) for piece in mine]


def scatter_row(parts):
    came = [shift(piece, "core", 1) for piece in parts[8:]]
    own, z0, p1, m1, p2, mz, pz, far = [added(a, b) for a, b in zip(parts[:8], came)]
    half = own.shape[0] // 2
    top = shift(far[:half], "x", -1)
    low = shift(far[half:], "x", 1)
    pz = jnp.concatenate([added(pz[:half], top), pz[half:]], 0)
    mz = jnp.concatenate([mz[:half], added(mz[half:], low)], 0)
    from_p2, from_mz, from_pz = shift(p2, "x", -1), shift(mz, "x", 1), shift(pz, "zl", 1)
    p1 = added(p1, from_p2, from_pz)
    z0 = added(z0, from_mz)
    return total(own, shift(p1, "x", -1), shift(m1, "x", 1), shift(z0, "zl", 1))


def gather_col(own):
    half = own.shape[0] // 2

    def along_y(piece):
        up, down = shift(piece, "y", 1), shift(piece, "y", -1)
        return [piece, up, down, shift(up[:half], "y", 1), shift(down[half:], "y", -1)]

    zp, zm = shift(own, "zh", 1), shift(own, "zh", -1)
    first = along_y(own)
    z2t, z2b = shift(zp[:half], "zh", 1), shift(zm[half:], "zh", -1)
    second, third = along_y(zp), along_y(zm)
    tu, td = shift(z2t, "y", 1), shift(z2t, "y", -1)
    bu, bd = shift(z2b, "y", 1), shift(z2b, "y", -1)
    last = [z2t, z2b, tu, bu, td, bd, shift(tu, "y", 1), shift(bd, "y", -1)]
    return first + second + third + last


def scatter_col(parts):
    half = -(-parts[0].shape[0] // 32) * 16

    def along_y(own, up, down, far):
        top, low = shift(far[:half], "y", -1), shift(far[half:], "y", 1)
        up = jnp.concatenate([added(up[:half], top), up[half:]], 0)
        down = jnp.concatenate([down[:half], added(down[half:], low)], 0)
        return added(own, shift(up, "y", -1), shift(down, "y", 1))

    far = along_y(*parts[12:])
    top, low = shift(far[:half], "zh", -1), shift(far[half:], "zh", 1)
    up, down = along_y(*parts[4:8]), along_y(*parts[8:12])
    up = jnp.concatenate([added(up[:half], top), up[half:]], 0)
    down = jnp.concatenate([down[:half], added(down[half:], low)], 0)
    from_up, from_down = shift(up, "zh", -1), shift(down, "zh", 1)
    return total(along_y(*parts[:4]), from_up, from_down)


def sum_all(piece):
    rows = piece.shape[1]
    x, zl, core = coordinate("x"), coordinate("zl"), coordinate("core")
    cube = piece.reshape(4, 2, 2, rows, F)

    def at(value, index, axis):
        return lax.dynamic_index_in_dim(value, index, axis, keepdims=False)

    cube = at(cube, core, 2) + shift(at(cube, 1 - core, 2), "core", 1)
    cube = at(cube, zl, 1) + shift(at(cube, 1 - zl, 1), "zl", 1)
    here = at(cube, x, 0)
    for step in (1, 2, 3):
        here = here + shift(at(cube, (x + step) % 4, 0), "x", step)
    for axis in ("y", "zh"):
        here = here + shift(here, axis, 1) + shift(here, axis, 2) + shift(here, axis, 3)
    ring = [here] + [shift(here, "x", step) for step in (1, 2, 3)]
    ring = jnp.stack(ring[::-1] * 2)
    slab = lax.dynamic_slice_in_dim(ring, 3 - x, 4, 0)
    other = shift(slab, "zl", 1)
    first = jnp.where(zl == 0, slab, other)
    slab = jnp.stack([first, jnp.where(zl == 0, other, slab)], 1)
    other = shift(slab, "core", 1)
    first = jnp.where(core == 0, slab, other)
    slab = jnp.stack([first, jnp.where(core == 0, other, slab)], 2)
    return slab.reshape(16, rows, F)


def degree_kernel(targets, tiles, out, sums):
    step, group = pl.program_id(0), tiles.shape[0]

    @pl.when(step == 0)
    def _():
        def clear(block, carried):
            sums[block] = jnp.zeros((BLK, BLK), f32)
            return carried

        lax.fori_loop(0, BLOCKS, clear, 0)

    def four(index, carried):
        for u in range(4):
            slot = index * 4 + u
            sums[targets[step * group + slot]] += tiles[slot].astype(f32)
        return carried

    lax.fori_loop(0, group // 4, four, 0)

    @pl.when(step == pl.num_programs(0) - 1)
    def _():
        for block in range(0, BLOCKS, 8):
            out[block : block + 8, :] = jnp.sum(sums[block : block + 8], axis=2)


def degrees(targets, tiles):
    group = SLOTS // PARTS
    return pl.pallas_call(
        degree_kernel,
        out_shape=jax.ShapeDtypeStruct((BLOCKS, BLK), f32),
        grid=(PARTS,),
        in_specs=[
            pl.BlockSpec(memory_space=pltpu.SMEM),
            pl.BlockSpec((group, BLK, BLK), lambda step: (step, 0, 0)),
        ],
        out_specs=pl.BlockSpec((BLOCKS, BLK), lambda step: (0, 0)),
        scratch_shapes=[pltpu.VMEM((BLOCKS + 1, BLK, BLK), f32)],
        compiler_params=pltpu.CompilerParams(vmem_limit_bytes=16 * 2**20),
        cost_estimate=pl.CostEstimate(
            flops=2 * SLOTS * BLK * BLK, bytes_accessed=8 * 2**20, transcendentals=0
        ),
        name="degrees",
    )(targets, tiles)


def product_kernel(transposed, starts, sources, targets, *refs):
    count = len(starts)
    chunks, tiles, refs = refs[:count], refs[count], refs[count + 1 :]
    extra = None if transposed else refs[0]
    refs = refs if transposed else refs[1:]
    outs, (panel, held, sums, chunk_sems, tile_sems) = refs[:16], refs[16:]
    part = SLOTS // PARTS
    tile_copies = []
    for i in range(PARTS):
        span = pl.ds(i * part, part)
        copy = pltpu.make_async_copy(tiles.at[span], held.at[span], tile_sems.at[i])
        tile_copies.append(copy)
    chunk_copies = []
    for i, (chunk, start) in enumerate(zip(chunks, starts)):
        span = pl.ds(start, chunk.shape[0])
        chunk_copies.append(pltpu.make_async_copy(chunk, panel.at[span], chunk_sems.at[i]))
    for copy in chunk_copies + tile_copies:
        copy.start()

    def clear(block, carried):
        sums[block] = jnp.zeros((BLK, F), f32)
        return carried

    lax.fori_loop(0, BLOCKS, clear, 0)
    for copy in chunk_copies:
        copy.wait()
    dims = (((0,), (0,)), ((), ())) if transposed else (((1,), (0,)), ((), ()))

    def group(index, carried):
        for u in range(UNROLL):
            slot = index * UNROLL + u
            start = pl.multiple_of(sources[slot] * BLK, BLK)
            block = panel[pl.ds(start, BLK), :]
            sums[targets[slot]] += lax.dot_general(
                held[slot], block, dims, preferred_element_type=f32
            )
        return carried

    steps = part // UNROLL
    for i in range(PARTS):
        tile_copies[i].wait()
        lax.fori_loop(i * steps, (i + 1) * steps, group, 0)
    per = CHUNK // BLK
    for j in range(16):
        for b in range(per):
            outs[j][b * BLK : (b + 1) * BLK, :] = sums[j * per + b].astype(bf16)
        if extra is not None:
            outs[j][CHUNK:, :] = extra[j]


def products(transposed, sources, targets, chunks, tiles, extra=None):
    starts, place = [], 0
    for chunk in chunks:
        starts.append(place)
        place += chunk.shape[0]
    rows = CHUNK + (0 if extra is None else extra.shape[1])
    scalars, whole = pl.BlockSpec(memory_space=pltpu.SMEM), pl.BlockSpec(memory_space=pltpu.VMEM)
    anywhere = pl.BlockSpec(memory_space=pl.ANY)
    extras = [] if extra is None else [extra]
    return pl.pallas_call(
        functools.partial(product_kernel, transposed, tuple(starts)),
        out_shape=[jax.ShapeDtypeStruct((rows, F), bf16)] * 16,
        in_specs=[scalars, scalars] + [anywhere] * (len(chunks) + 1) + [whole] * len(extras),
        out_specs=[whole] * 16,
        scratch_shapes=[
            pltpu.VMEM((BLOCKS * BLK, F), bf16),
            pltpu.VMEM((SLOTS, BLK, BLK), bf16),
            pltpu.VMEM((BLOCKS + 1, BLK, F), f32),
            pltpu.SemaphoreType.DMA((len(chunks),)),
            pltpu.SemaphoreType.DMA((PARTS,)),
        ],
        compiler_params=pltpu.CompilerParams(vmem_limit_bytes=40 * 2**20),
        cost_estimate=pl.CostEstimate(
            flops=2 * SLOTS * BLK * BLK * F, bytes_accessed=16 * 2**20, transcendentals=0
        ),
        name="products_back" if transposed else "products",
    )(sources, targets, *chunks, tiles, *extras)


def shards(
    features,
    cotangent,
    w_self,
    w_neigh,
    bias_term,
    block_tiles,
    block_rows,
    block_cols,
    block_counts,
):
    tiles, rows, cols = block_tiles[0, 0], block_rows[0, 0], block_cols[0, 0]
    live = jnp.arange(SLOTS) < block_counts[0, 0]
    x, zl, core = coordinate("x"), coordinate("zl"), coordinate("core")
    zh, y = coordinate("zh"), coordinate("y")
    place = 2 * ((cols // 16 - x) % 4) + (cols // 8 - zl) % 2
    col_ids = (look_up(PLANE_PLACE, place) + 8 * ((cols // 4 - core) % 2)) * 4 + cols % 4
    place = 4 * look_up(RING_PLACE, (rows // 16 - zh) % 4)
    row_ids = (place + look_up(RING_PLACE, (rows // 4 - y) % 4)) * 4 + rows % 4
    row_targets = jnp.where(live, row_ids, BLOCKS)
    col_targets = jnp.where(live, col_ids, BLOCKS)

    source_panel = gather_row(features)
    partial_degree = degrees(row_targets, tiles)
    extra = jnp.pad(partial_degree.reshape(16, 2, F), ((0, 0), (0, 14), (0, 0))).astype(bf16)
    partial = products(False, col_ids, row_targets, source_panel, tiles, extra)
    whole = scatter_col(partial)
    aggregate, degree = whole[:CHUNK], whole[CHUNK : CHUNK + 2].reshape(CHUNK)

    scale = lax.rsqrt(1.0 + degree)
    neigh = (scale[:, None] * aggregate).astype(bf16)
    pre = (
        jnp.dot(features, w_self, preferred_element_type=f32)
        + jnp.dot(neigh, w_neigh, preferred_element_type=f32)
        + bias_term.astype(f32)
    )
    sigma = jax.nn.sigmoid(pre)
    activation = (pre * sigma).astype(bf16)
    dpre = (cotangent.astype(f32) * sigma * (1.0 + pre * (1.0 - sigma))).astype(bf16)
    contract_cols = (((1,), (1,)), ((), ()))
    back = (
        scale[:, None] * lax.dot_general(dpre, w_neigh, contract_cols, preferred_element_type=f32)
    ).astype(bf16)
    dest_panel = gather_col(back)

    contract_rows = (((0,), (0,)), ((), ()))
    local_self = lax.dot_general(features, dpre, contract_rows, preferred_element_type=f32)
    local_neigh = lax.dot_general(neigh, dpre, contract_rows, preferred_element_type=f32)
    local_bias = jnp.sum(dpre.astype(f32), axis=0)
    local = jnp.concatenate([local_self, local_neigh], 0).reshape(16, 32, F)
    mine = jnp.arange(16) == lax.axis_index("row")
    local_bias = jnp.where(mine[:, None], local_bias[None, :], 0.0)
    local = jnp.concatenate([local, jnp.pad(local_bias[:, None], ((0, 0), (0, 7), (0, 0)))], 1)
    grads = sum_all(local) * (1.0 / jnp.sqrt(f32(CHUNK * 256)))
    weights = grads[:, :32].reshape(2, F, F)

    partial_src = products(True, row_ids, col_targets, dest_panel, tiles)
    own_term = lax.dot_general(dpre, w_self, contract_cols, preferred_element_type=f32)
    grad_features = (own_term + scatter_row(partial_src)).astype(bf16)
    return activation, grad_features, weights[0], weights[1], jnp.sum(grads[:, 32], axis=0)


def solution(mesh):
    return jax.shard_map(
        shards,
        mesh=mesh,
        in_specs=(
            P(("row", "col"), None),
            P(("row", "col"), None),
            P(),
            P(),
            P(),
            P("row", "col", None, None, None),
            P("row", "col", None),
            P("row", "col", None),
            P("row", "col"),
        ),
        out_specs=(P(("row", "col"), None), P(("row", "col"), None), P(), P(), P()),
        check_vma=False,
    )
```

```python
import functools

import jax
import jax.numpy as jnp
from jax import lax
from jax.experimental import pallas as pl
from jax.experimental.pallas import tpu as pltpu
from jax.sharding import PartitionSpec as P

f32, bf16 = jnp.float32, jnp.bfloat16
BLK, F, SLOTS, BLOCKS = 128, 256, 256, 64
CHUNK = 512
HALF = CHUNK // 2
PARTS = 8
UNROLL = 16

GRIDS = {
    "x": ("row", 4, 4),
    "zl": ("row", 2, 2),
    "core": ("row", 2, 1),
    "zh": ("col", 4, 4),
    "y": ("col", 4, 1),
}
RING_PLACE = (0, 2, 3, 1)
PLANE_PLACE = (0, 1, 3, 5, 4, 7, 2, 6)


def coordinate(axis):
    name, size, stride = GRIDS[axis]
    return lax.axis_index(name) // stride % size


def shift(value, axis, step):
    name, size, stride = GRIDS[axis]
    pairs = []
    for source in range(16):
        at = source // stride % size
        pairs.append((source, source + ((at + step) % size - at) * stride))
    return lax.ppermute(value, name, pairs)


def exchange(value, axis, partner):
    name, size, stride = GRIDS[axis]
    pairs = []
    for source in range(16):
        at = source // stride % size
        pairs.append((source, source + (partner[at] - at) * stride))
    return lax.ppermute(value, name, pairs)


def total(*terms):
    out = terms[0].astype(f32)
    for term in terms[1:]:
        out = out + term.astype(f32)
    return out


def added(*terms):
    return total(*terms).astype(bf16)


def look_up(table, index):
    out = jnp.zeros_like(index)
    for place, entry in enumerate(table):
        out = jnp.where(index == place, entry, out)
    return out


def after(values, *others):
    return lax.optimization_barrier((tuple(values), others))[0]


def add_top(value, piece):
    half = piece.shape[0]
    return jnp.concatenate([added(value[:half], piece), value[half:]], 0)


def add_low(value, piece):
    half = value.shape[0] - piece.shape[0]
    return jnp.concatenate([value[:half], added(value[half:], piece)], 0)


def gather_row(own, beside):
    z0 = shift(own, "zl", 1)
    p1, m1 = shift(own, "x", 1), shift(own, "x", -1)
    p1, z0, m1 = after((p1, z0, m1), beside)
    pz = shift(p1, "zl", 1)
    p2 = shift(p1, "x", 1)
    mz = shift(z0, "x", -1)
    top = shift(pz[:HALF], "x", 1)
    low = shift(mz[HALF:], "x", -1)
    mine = [own, z0, p1, m1, p2, mz, pz, top, low]
    return mine + [shift(piece, "core", 1) for piece in mine]


ROW_PARTS = [[(i, 0, CHUNK)] for i in range(16)]


def scatter_row(parts, grads):
    (far,) = grads.step(added(parts[7], shift(parts[15], "core", 1)))
    top, low = shift(far[:HALF], "x", -1), shift(far[HALF:], "x", 1)
    came = [shift(part, "core", 1) for part in parts[8:15]]
    own, z0, p1, m1, p2, mz, pz = [added(part, piece) for part, piece in zip(parts[:7], came)]
    pz, mz = grads.step(add_top(pz, top), add_low(mz, low))
    from_p2, from_mz, from_pz = shift(p2, "x", -1), shift(mz, "x", 1), shift(pz, "zl", 1)
    p1, z0 = grads.step(added(p1, from_p2, from_pz), added(z0, from_mz))
    return total(own, shift(p1, "x", -1), shift(m1, "x", 1), shift(z0, "zl", 1))


def gather_col(own, grads):
    rows, half = own.shape[0], own.shape[0] // 2
    zp, zm = shift(own, "zh", 1), shift(own, "zh", -1)
    up, down = shift(own, "y", 1), shift(own, "y", -1)
    y2t, y2b = shift(up[:half], "y", 1), shift(down[half:], "y", -1)
    grads.start(up, down)
    y2t, y2b = grads.step(y2t, y2b)
    zp, zm = grads.step(zp, zm)
    pair = jnp.concatenate([zp, zm], 0)
    z2t, z2b = shift(zp[:half], "zh", 1), shift(zm[half:], "zh", -1)
    pair_up, pair_down = shift(pair, "y", 1), shift(pair, "y", -1)
    y2 = jnp.concatenate([y2t, y2b], 0)
    z2 = jnp.concatenate([z2t, z2b], 0)
    z2, y2 = grads.step(z2, y2)
    far_up, far_down = shift(y2, "zh", 1), shift(y2, "zh", -1)
    z2_up, z2_down = shift(z2, "y", 1), shift(z2, "y", -1)
    pair_up, pair_down = grads.step(pair_up, pair_down)
    z2_up, z2_down = grads.step(z2_up, z2_down)
    last_t, last_b = shift(z2_up[:half], "y", 1), shift(z2_down[half:], "y", -1)
    last_t, last_b = grads.step(last_t, last_b)
    places = [(own, 0), (up, 1), (down, 2), (y2, 3), (zp, 4), (far_up, 7), (zm, 8), (far_down, 11)]
    places += [(z2, 12), (z2_up, 13), (z2_down, 14)]
    places = [(piece, 0, rows, at * CHUNK) for piece, at in places]
    for piece, at in ((pair_up, 5), (pair_down, 6)):
        places += [(piece, 0, rows, at * CHUNK), (piece, rows, rows, (at + 4) * CHUNK)]
    places += [(last_t, 0, half, 15 * CHUNK), (last_b, 0, half, 15 * CHUNK + half)]
    return places


WIDE = CHUNK + 16
COL_PARTS = [[(15, 0, HALF)], [(15, HALF, WIDE)], [(7, 0, WIDE)], [(11, 0, WIDE)]]
COL_PARTS += [[(5, 0, WIDE), (9, 0, WIDE)], [(6, 0, WIDE), (10, 0, WIDE)]]
COL_PARTS += [[(i, 0, WIDE)] for i in (13, 14, 12, 4, 8, 3, 1, 2, 0)]


def scatter_col(parts):
    last_t, last_b, far_up, far_down, pair_up, pair_down = parts[:6]
    z2_up, z2_down, z2, zp, zm, y2, up, down, own = parts[6:]
    half, rows = last_t.shape[0], own.shape[0]
    last_t, last_b = shift(last_t, "y", -1), shift(last_b, "y", 1)
    far_up, far_down = shift(far_up, "zh", -1), shift(far_down, "zh", 1)
    pair_up, pair_down = shift(pair_up, "y", -1), shift(pair_down, "y", 1)
    z2_up = shift(add_top(z2_up, last_t), "y", -1)
    z2_down = shift(add_low(z2_down, last_b), "y", 1)
    z2 = added(z2, z2_up, z2_down)
    y2 = added(y2, far_up, far_down)
    z2, y2 = after((z2, y2))
    z2t, z2b = shift(z2[:half], "zh", -1), shift(z2[half:], "zh", 1)
    zp = added(zp, pair_up[:rows], pair_down[:rows])
    zm = added(zm, pair_up[rows:], pair_down[rows:])
    y2, zp, zm = after((y2, zp, zm))
    y2t, y2b = shift(y2[:half], "y", -1), shift(y2[half:], "y", 1)
    zp, zm = shift(add_top(zp, z2t), "zh", -1), shift(add_low(zm, z2b), "zh", 1)
    up, down = shift(add_top(up, y2t), "y", -1), shift(add_low(down, y2b), "y", 1)
    return total(own, up, down, zp, zm)


class Sums:
    def __init__(self, make, *values):
        self.make, self.values = make, values

    def start(self, *others):
        self.steps = self.run(self.make(*after(self.values, *others)))
        self.now = next(self.steps)

    def step(self, *others):
        now, others = lax.optimization_barrier((self.now, others))
        self.now = self.steps.send(now)
        return others

    def run(self, piece):
        zl, core = coordinate("zl"), coordinate("core")

        def at(value, index):
            return lax.dynamic_index_in_dim(value, index, 0, keepdims=False)

        def both(mine, other, index):
            first = jnp.where(index == 0, mine, other)
            return jnp.concatenate([first, jnp.where(index == 0, other, mine)], 0)

        halves = piece.reshape(2, -1, F)
        (came,) = yield (shift(at(halves, 1 - core), "core", 1),)
        halves = (at(halves, core) + came).reshape(2, -1, F)
        (came,) = yield (shift(at(halves, 1 - zl), "zl", 1),)
        here = at(halves, zl) + came
        for axis in ("x", "y", "zh"):
            for partner in (1, 0, 3, 2), (3, 2, 1, 0):
                (came,) = yield (exchange(here, axis, partner),)
                here = here + came
        (came,) = yield (shift(here, "zl", 1),)
        here = both(here, came, zl)
        (came,) = yield (shift(here, "core", 1),)
        yield both(here, came, core)


def degree_kernel(targets, tiles, out, held, sums, sems):
    part = SLOTS // PARTS
    copies = []
    for i in range(PARTS):
        span = pl.ds(i * part, part)
        copies.append(pltpu.make_async_copy(tiles.at[span], held.at[span], sems.at[i]))
    for copy in copies:
        copy.start()

    def clear(block, carried):
        sums[block] = jnp.zeros((BLK, BLK), f32)
        return carried

    lax.fori_loop(0, BLOCKS, clear, 0)

    def four(index, carried):
        for u in range(4):
            slot = index * 4 + u
            sums[targets[slot]] += held[slot].astype(f32)
        return carried

    for i in range(PARTS):
        copies[i].wait()
        lax.fori_loop(i * part // 4, (i + 1) * part // 4, four, 0)
    for block in range(0, BLOCKS, 8):
        out[block : block + 8, :] = jnp.sum(sums[block : block + 8], axis=2)


def degrees(targets, tiles):
    return pl.pallas_call(
        degree_kernel,
        out_shape=jax.ShapeDtypeStruct((BLOCKS, BLK), f32),
        in_specs=[
            pl.BlockSpec(memory_space=pltpu.SMEM),
            pl.BlockSpec(memory_space=pl.ANY),
        ],
        out_specs=pl.BlockSpec(memory_space=pltpu.VMEM),
        scratch_shapes=[
            pltpu.VMEM((SLOTS, BLK, BLK), bf16),
            pltpu.VMEM((BLOCKS + 1, BLK, BLK), f32),
            pltpu.SemaphoreType.DMA((PARTS,)),
        ],
        compiler_params=pltpu.CompilerParams(vmem_limit_bytes=54 * 2**20),
        cost_estimate=pl.CostEstimate(
            flops=2 * SLOTS * BLK * BLK, bytes_accessed=8 * 2**20, transcendentals=0
        ),
        name="degrees",
    )(targets, tiles)


def product_kernel(transposed, spans, out_parts, sources, targets, tiles, *refs):
    count = 1 + max(span[0] for span in spans)
    chunks, refs = refs[:count], refs[count:]
    extra = None if transposed else refs[0]
    refs = refs if transposed else refs[1:]
    outs, refs = refs[: len(out_parts)], refs[len(out_parts) :]
    panel, held, sums, sems, tile_sems = refs
    part, tile_copies, copies = SLOTS // PARTS, [], []
    for i in range(PARTS):
        span = pl.ds(i * part, part)
        copy = pltpu.make_async_copy(tiles.at[span], held.at[span], tile_sems.at[i])
        tile_copies.append(copy)
    for i, (chunk, first, rows, place) in enumerate(spans):
        source = chunks[chunk].at[pl.ds(first, rows)]
        copies.append(pltpu.make_async_copy(source, panel.at[pl.ds(place, rows)], sems.at[i]))
    for copy in copies + tile_copies:
        copy.start()

    def clear(block, carried):
        sums[block] = jnp.zeros((BLK, F), f32)
        return carried

    lax.fori_loop(0, BLOCKS, clear, 0)
    for copy in copies:
        copy.wait()
    dims = (((0,), (0,)), ((), ())) if transposed else (((1,), (0,)), ((), ()))

    def group(index, carried):
        for u in range(UNROLL):
            slot = index * UNROLL + u
            start = pl.multiple_of(sources[slot] * BLK, BLK)
            block = panel[pl.ds(start, BLK), :]
            sums[targets[slot]] += lax.dot_general(
                held[slot], block, dims, preferred_element_type=f32
            )
        return carried

    for i in range(PARTS):
        tile_copies[i].wait()
        lax.fori_loop(i * part // UNROLL, (i + 1) * part // UNROLL, group, 0)
    for out, part in zip(outs, out_parts):
        place = 0
        for chunk, first, last in part:
            for row in range(first, min(last, CHUNK), BLK):
                block = sums[chunk * (CHUNK // BLK) + row // BLK]
                out[place : place + BLK, :] = block.astype(bf16)
                place += BLK
            if last > CHUNK:
                out[place : place + last - CHUNK, :] = extra[chunk]
                place += last - CHUNK


def products(transposed, sources, targets, pieces, out_parts, tiles, extra=None):
    arrays, spans = [], []
    for array, first, rows, place in pieces:
        known = [i for i, other in enumerate(arrays) if other is array]
        if not known:
            known = [len(arrays)]
            arrays.append(array)
        spans.append((known[0], first, rows, place))
    scalars, whole = pl.BlockSpec(memory_space=pltpu.SMEM), pl.BlockSpec(memory_space=pltpu.VMEM)
    anywhere = pl.BlockSpec(memory_space=pl.ANY)
    extras = [] if extra is None else [extra]
    sizes = [sum(last - first for _, first, last in part) for part in out_parts]
    return pl.pallas_call(
        functools.partial(product_kernel, transposed, tuple(spans), out_parts),
        out_shape=[jax.ShapeDtypeStruct((rows, F), bf16) for rows in sizes],
        in_specs=[scalars, scalars, anywhere] + [anywhere] * len(arrays) + [whole] * len(extras),
        out_specs=[whole] * len(sizes),
        scratch_shapes=[
            pltpu.VMEM((BLOCKS * BLK, F), bf16),
            pltpu.VMEM((SLOTS, BLK, BLK), bf16),
            pltpu.VMEM((BLOCKS + 1, BLK, F), f32),
            pltpu.SemaphoreType.DMA((len(spans),)),
            pltpu.SemaphoreType.DMA((PARTS,)),
        ],
        compiler_params=pltpu.CompilerParams(vmem_limit_bytes=48 * 2**20),
        cost_estimate=pl.CostEstimate(
            flops=2 * SLOTS * BLK * BLK * F, bytes_accessed=16 * 2**20, transcendentals=0
        ),
        name="products_back" if transposed else "products",
    )(sources, targets, tiles, *arrays, *extras)


def shards(
    features,
    cotangent,
    w_self,
    w_neigh,
    bias_term,
    block_tiles,
    block_rows,
    block_cols,
    block_counts,
):
    tiles, rows, cols = block_tiles[0, 0], block_rows[0, 0], block_cols[0, 0]
    live = jnp.arange(SLOTS) < block_counts[0, 0]
    x, zl, core = coordinate("x"), coordinate("zl"), coordinate("core")
    zh, y = coordinate("zh"), coordinate("y")
    place = 2 * ((cols // 16 - x) % 4) + (cols // 8 - zl) % 2
    col_ids = (look_up(PLANE_PLACE, place) + 8 * ((cols // 4 - core) % 2)) * 4 + cols % 4
    place = 4 * look_up(RING_PLACE, (rows // 16 - zh) % 4)
    row_ids = (place + look_up(RING_PLACE, (rows // 4 - y) % 4)) * 4 + rows % 4
    row_targets = jnp.where(live, row_ids, BLOCKS)
    col_targets = jnp.where(live, col_ids, BLOCKS)


    extra = degrees(row_targets, tiles).reshape(16, 2, F)
    extra = jnp.pad(extra, ((0, 0), (0, 14), (0, 0))).astype(bf16)
    pieces, place = [], 0
    for chunk in gather_row(features, extra):
        pieces.append((chunk, 0, chunk.shape[0], place))
        place += chunk.shape[0]
    whole = scatter_col(products(False, col_ids, row_targets, pieces, COL_PARTS, tiles, extra))
    aggregate, degree = whole[:CHUNK], whole[CHUNK : CHUNK + 2].reshape(CHUNK)

    scale = lax.rsqrt(1.0 + degree)
    neigh = (scale[:, None] * aggregate).astype(bf16)
    pre = (
        jnp.dot(features, w_self, preferred_element_type=f32)
        + jnp.dot(neigh, w_neigh, preferred_element_type=f32)
        + bias_term.astype(f32)
    )
    sigma = jax.nn.sigmoid(pre)
    activation = (pre * sigma).astype(bf16)
    dpre = (cotangent.astype(f32) * sigma * (1.0 + pre * (1.0 - sigma))).astype(bf16)
    contract_cols = (((1,), (1,)), ((), ()))
    back = (
        scale[:, None] * lax.dot_general(dpre, w_neigh, contract_cols, preferred_element_type=f32)
    ).astype(bf16)

    def local_grads(features, neigh, dpre):
        contract_rows = (((0,), (0,)), ((), ()))
        local_self = lax.dot_general(features, dpre, contract_rows, preferred_element_type=f32)
        local_neigh = lax.dot_general(neigh, dpre, contract_rows, preferred_element_type=f32)
        local_bias = jnp.sum(dpre.astype(f32), axis=0)
        local_bias = jnp.pad(local_bias[None], ((0, 31), (0, 0)))
        return jnp.concatenate([local_self, local_neigh, local_bias], 0)

    grads = Sums(local_grads, features, neigh, dpre)
    pieces = gather_col(back, grads)
    partial_src = products(True, row_ids, col_targets, pieces, ROW_PARTS, tiles)
    own_term = lax.dot_general(dpre, w_self, contract_cols, preferred_element_type=f32)
    grad_features = (own_term + scatter_row(partial_src, grads)).astype(bf16)
    grads.step()
    grads = grads.now * (1.0 / jnp.sqrt(f32(CHUNK * 256)))
    return activation, grad_features, grads[:F], grads[F : 2 * F], grads[2 * F]


def solution(mesh):
    return jax.shard_map(
        shards,
        mesh=mesh,
        in_specs=(
            P(("row", "col"), None),
            P(("row", "col"), None),
            P(),
            P(),
            P(),
            P("row", "col", None, None, None),
            P("row", "col", None),
            P("row", "col", None),
            P("row", "col"),
        ),
        out_specs=(P(("row", "col"), None), P(("row", "col"), None), P(), P(), P()),
        check_vma=False,
    )
```

```python
import functools

import jax
import jax.numpy as jnp
from jax import lax
from jax.experimental import pallas as pl
from jax.experimental.pallas import tpu as pltpu
from jax.sharding import PartitionSpec as P

f32, bf16 = jnp.float32, jnp.bfloat16
BLK, F, SLOTS, BLOCKS = 128, 256, 256, 64
CHUNK = 512
HALF = CHUNK // 2
PARTS = 4
UNROLL = 64

GRIDS = {
    "x": ("row", 4, 4),
    "zl": ("row", 2, 2),
    "core": ("row", 2, 1),
    "zh": ("col", 4, 4),
    "y": ("col", 4, 1),
}
RING_PLACE = (0, 2, 3, 1)
PLANE_PLACE = (0, 1, 3, 5, 4, 7, 2, 6)


def coordinate(axis):
    name, size, stride = GRIDS[axis]
    return lax.axis_index(name) // stride % size


def shift(value, axis, step):
    name, size, stride = GRIDS[axis]
    pairs = []
    for source in range(16):
        at = source // stride % size
        pairs.append((source, source + ((at + step) % size - at) * stride))
    return lax.ppermute(value, name, pairs)


def exchange(value, axis, partner):
    name, size, stride = GRIDS[axis]
    pairs = []
    for source in range(16):
        at = source // stride % size
        pairs.append((source, source + (partner[at] - at) * stride))
    return lax.ppermute(value, name, pairs)


def total(*terms):
    out = terms[0].astype(f32)
    for term in terms[1:]:
        out = out + term.astype(f32)
    return out


def added(*terms):
    return total(*terms).astype(bf16)


def look_up(table, index):
    out = jnp.zeros_like(index)
    for place, entry in enumerate(table):
        out = jnp.where(index == place, entry, out)
    return out


def after(values, *others):
    return lax.optimization_barrier((tuple(values), others))[0]


def add_top(value, piece):
    half = piece.shape[0]
    return jnp.concatenate([added(value[:half], piece), value[half:]], 0)


def add_low(value, piece):
    half = value.shape[0] - piece.shape[0]
    return jnp.concatenate([value[:half], added(value[half:], piece)], 0)


def gather_row(own, beside):
    z0 = shift(own, "zl", 1)
    p1, m1 = shift(own, "x", 1), shift(own, "x", -1)
    p1, z0, m1 = after((p1, z0, m1), beside)
    pz = shift(p1, "zl", 1)
    p2 = shift(p1, "x", 1)
    mz = shift(z0, "x", -1)
    top = shift(pz[:HALF], "x", 1)
    low = shift(mz[HALF:], "x", -1)
    mine = [own, z0, p1, m1, p2, mz, pz, top, low]
    return mine + [shift(piece, "core", 1) for piece in mine]


ROW_PARTS = [[(i, 0, CHUNK)] for i in range(16)]


def scatter_row(parts, grads):
    far = added(parts[7], shift(parts[15], "core", 1))
    top, low = shift(far[:HALF], "x", -1), shift(far[HALF:], "x", 1)
    came = [shift(part, "core", 1) for part in parts[8:15]]
    own, z0, p1, m1, p2, mz, pz = [added(part, piece) for part, piece in zip(parts[:7], came)]
    pz, mz = grads.step(add_top(pz, top), add_low(mz, low))
    from_p2, from_mz, from_pz = shift(p2, "x", -1), shift(mz, "x", 1), shift(pz, "zl", 1)
    p1, z0 = grads.step(added(p1, from_p2, from_pz), added(z0, from_mz))
    return total(own, shift(p1, "x", -1), shift(m1, "x", 1), shift(z0, "zl", 1))


def gather_col(own, grads):
    rows, half = own.shape[0], own.shape[0] // 2
    zp, zm = shift(own, "zh", 1), shift(own, "zh", -1)
    up, down = shift(own, "y", 1), shift(own, "y", -1)
    grads.start()
    zp, zm, up, down = grads.step(zp, zm, up, down)
    y2t, y2b = shift(up[:half], "y", 1), shift(down[half:], "y", -1)
    y2t, y2b = grads.step(y2t, y2b)
    pair = jnp.concatenate([zp, zm], 0)
    z2t, z2b = shift(zp[:half], "zh", 1), shift(zm[half:], "zh", -1)
    pair_up, pair_down = shift(pair, "y", 1), shift(pair, "y", -1)
    y2 = jnp.concatenate([y2t, y2b], 0)
    z2 = jnp.concatenate([z2t, z2b], 0)
    z2, y2 = grads.step(z2, y2)
    far_up, far_down = shift(y2, "zh", 1), shift(y2, "zh", -1)
    z2_up, z2_down = shift(z2, "y", 1), shift(z2, "y", -1)
    pair_up, pair_down = grads.step(pair_up, pair_down)
    z2_up, z2_down = grads.step(z2_up, z2_down)
    last_t, last_b = shift(z2_up[:half], "y", 1), shift(z2_down[half:], "y", -1)
    last_t, last_b = grads.step(last_t, last_b)
    places = [(own, 0), (up, 1), (down, 2), (y2, 3), (zp, 4), (far_up, 7), (zm, 8), (far_down, 11)]
    places += [(z2, 12), (z2_up, 13), (z2_down, 14)]
    places = [(piece, 0, rows, at * CHUNK) for piece, at in places]
    for piece, at in ((pair_up, 5), (pair_down, 6)):
        places += [(piece, 0, rows, at * CHUNK), (piece, rows, rows, (at + 4) * CHUNK)]
    places += [(last_t, 0, half, 15 * CHUNK), (last_b, 0, half, 15 * CHUNK + half)]
    return places


WIDE = CHUNK + 16
COL_PARTS = [[(15, 0, HALF)], [(15, HALF, WIDE)], [(7, 0, WIDE)], [(11, 0, WIDE)]]
COL_PARTS += [[(5, 0, WIDE), (9, 0, WIDE)], [(6, 0, WIDE), (10, 0, WIDE)]]
COL_PARTS += [[(i, 0, WIDE)] for i in (13, 14, 12, 4, 8, 3, 1, 2, 0)]


def scatter_col(parts):
    last_t, last_b, far_up, far_down, pair_up, pair_down = parts[:6]
    z2_up, z2_down, z2, zp, zm, y2, up, down, own = parts[6:]
    half, rows = last_t.shape[0], own.shape[0]
    last_t, last_b = after((shift(last_t, "y", -1), shift(last_b, "y", 1)))
    far_up, far_down = shift(far_up, "zh", -1), shift(far_down, "zh", 1)
    pair_up, pair_down = shift(pair_up, "y", -1), shift(pair_down, "y", 1)
    z2_up = shift(add_top(z2_up, last_t), "y", -1)
    z2_down = shift(add_low(z2_down, last_b), "y", 1)
    z2 = added(z2, z2_up, z2_down)
    y2 = added(y2, far_up, far_down)
    z2, y2 = after((z2, y2))
    z2t, z2b = shift(z2[:half], "zh", -1), shift(z2[half:], "zh", 1)
    zp = added(zp, pair_up[:rows], pair_down[:rows])
    zm = added(zm, pair_up[rows:], pair_down[rows:])
    y2, zp, zm = after((y2, zp, zm))
    y2t, y2b = shift(y2[:half], "y", -1), shift(y2[half:], "y", 1)
    zp, zm = shift(add_top(zp, z2t), "zh", -1), shift(add_low(zm, z2b), "zh", 1)
    up, down = shift(add_top(up, y2t), "y", -1), shift(add_low(down, y2b), "y", 1)
    return total(own, up, down, zp, zm)


class Sums:
    def __init__(self, make, *values):
        self.make, self.values = make, values

    def start(self, *others):
        self.steps = self.run(self.make(*after(self.values, *others)))
        self.now = next(self.steps)

    def step(self, *others):
        now, others = lax.optimization_barrier((self.now, others))
        self.now = self.steps.send(now)
        return others

    def run(self, piece):
        zl, core = coordinate("zl"), coordinate("core")

        def at(value, index):
            return lax.dynamic_index_in_dim(value, index, 0, keepdims=False)

        def both(mine, other, index):
            first = jnp.where(index == 0, mine, other)
            return jnp.concatenate([first, jnp.where(index == 0, other, mine)], 0)

        halves = piece.reshape(2, -1, F)
        (came,) = yield (shift(at(halves, 1 - core), "core", 1),)
        halves = (at(halves, core) + came).reshape(2, -1, F)
        (came,) = yield (shift(at(halves, 1 - zl), "zl", 1),)
        here = at(halves, zl) + came
        came = yield tuple(shift(here, "x", step) for step in (1, 2, 3))
        here = (here + came[1]) + (came[0] + came[2])
        for axis in ("y", "zh"):
            for partner in (1, 0, 3, 2), (3, 2, 1, 0):
                (came,) = yield (exchange(here, axis, partner),)
                here = here + came
        (came,) = yield (shift(here, "zl", 1),)
        here = both(here, came, zl)
        (came,) = yield (shift(here, "core", 1),)
        yield both(here, came, core)


def degree_kernel(targets, tiles, out, held, sums, sems):
    part = SLOTS // PARTS
    copies = []
    for i in range(PARTS):
        span = pl.ds(i * part, part)
        copies.append(pltpu.make_async_copy(tiles.at[span], held.at[span], sems.at[i]))
    for copy in copies:
        copy.start()

    def clear(block, carried):
        sums[block] = jnp.zeros((BLK, BLK), f32)
        return carried

    lax.fori_loop(0, BLOCKS, clear, 0)

    def four(index, carried):
        for u in range(4):
            slot = index * 4 + u
            sums[targets[slot]] += held[slot].astype(f32)
        return carried

    for i in range(PARTS):
        copies[i].wait()
        lax.fori_loop(i * part // 4, (i + 1) * part // 4, four, 0)
    for block in range(0, BLOCKS, 8):
        out[block : block + 8, :] = jnp.sum(sums[block : block + 8], axis=2)


def degrees(targets, tiles):
    return pl.pallas_call(
        degree_kernel,
        out_shape=jax.ShapeDtypeStruct((BLOCKS, BLK), f32),
        in_specs=[
            pl.BlockSpec(memory_space=pltpu.SMEM),
            pl.BlockSpec(memory_space=pl.ANY),
        ],
        out_specs=pl.BlockSpec(memory_space=pltpu.VMEM),
        scratch_shapes=[
            pltpu.VMEM((SLOTS, BLK, BLK), bf16),
            pltpu.VMEM((BLOCKS + 1, BLK, BLK), f32),
            pltpu.SemaphoreType.DMA((PARTS,)),
        ],
        compiler_params=pltpu.CompilerParams(vmem_limit_bytes=54 * 2**20),
        cost_estimate=pl.CostEstimate(
            flops=2 * SLOTS * BLK * BLK, bytes_accessed=8 * 2**20, transcendentals=0
        ),
        name="degrees",
    )(targets, tiles)


def product_kernel(transposed, spans, out_parts, sources, targets, tiles, *refs):
    count = 1 + max(span[0] for span in spans)
    chunks, refs = refs[:count], refs[count:]
    extra = None if transposed else refs[0]
    refs = refs if transposed else refs[1:]
    outs, refs = refs[: len(out_parts)], refs[len(out_parts) :]
    panel, held, sums, sems, tile_sems = refs
    part, tile_copies, copies = SLOTS // PARTS, [], []
    for i in range(PARTS):
        span = pl.ds(i * part, part)
        copy = pltpu.make_async_copy(tiles.at[span], held.at[span], tile_sems.at[i])
        tile_copies.append(copy)
    for i, (chunk, first, rows, place) in enumerate(spans):
        source = chunks[chunk].at[pl.ds(first, rows)]
        copies.append(pltpu.make_async_copy(source, panel.at[pl.ds(place, rows)], sems.at[i]))
    for copy in copies + tile_copies:
        copy.start()

    def clear(block, carried):
        sums[block] = jnp.zeros((BLK, F), f32)
        return carried

    lax.fori_loop(0, BLOCKS, clear, 0)
    for copy in copies:
        copy.wait()
    dims = (((0,), (0,)), ((), ())) if transposed else (((1,), (0,)), ((), ()))

    def group(index, carried):
        for u in range(UNROLL):
            slot = index * UNROLL + u
            start = pl.multiple_of(sources[slot] * BLK, BLK)
            block = panel[pl.ds(start, BLK), :]
            sums[targets[slot]] += lax.dot_general(
                held[slot], block, dims, preferred_element_type=f32
            )
        return carried

    for i in range(PARTS):
        tile_copies[i].wait()
        lax.fori_loop(i * part // UNROLL, (i + 1) * part // UNROLL, group, 0)
    for out, part in zip(outs, out_parts):
        place = 0
        for chunk, first, last in part:
            for row in range(first, min(last, CHUNK), BLK):
                block = sums[chunk * (CHUNK // BLK) + row // BLK]
                out[place : place + BLK, :] = block.astype(bf16)
                place += BLK
            if last > CHUNK:
                out[place : place + last - CHUNK, :] = extra[chunk]
                place += last - CHUNK


def products(transposed, sources, targets, pieces, out_parts, tiles, extra=None):
    arrays, spans = [], []
    for array, first, rows, place in pieces:
        known = [i for i, other in enumerate(arrays) if other is array]
        if not known:
            known = [len(arrays)]
            arrays.append(array)
        spans.append((known[0], first, rows, place))
    scalars, whole = pl.BlockSpec(memory_space=pltpu.SMEM), pl.BlockSpec(memory_space=pltpu.VMEM)
    anywhere = pl.BlockSpec(memory_space=pl.ANY)
    extras = [] if extra is None else [extra]
    sizes = [sum(last - first for _, first, last in part) for part in out_parts]
    return pl.pallas_call(
        functools.partial(product_kernel, transposed, tuple(spans), out_parts),
        out_shape=[jax.ShapeDtypeStruct((rows, F), bf16) for rows in sizes],
        in_specs=[scalars, scalars, anywhere] + [anywhere] * len(arrays) + [whole] * len(extras),
        out_specs=[whole] * len(sizes),
        scratch_shapes=[
            pltpu.VMEM((BLOCKS * BLK, F), bf16),
            pltpu.VMEM((SLOTS, BLK, BLK), bf16),
            pltpu.VMEM((BLOCKS + 1, BLK, F), f32),
            pltpu.SemaphoreType.DMA((len(spans),)),
            pltpu.SemaphoreType.DMA((PARTS,)),
        ],
        compiler_params=pltpu.CompilerParams(vmem_limit_bytes=48 * 2**20),
        cost_estimate=pl.CostEstimate(
            flops=2 * SLOTS * BLK * BLK * F, bytes_accessed=16 * 2**20, transcendentals=0
        ),
        name="products_back" if transposed else "products",
    )(sources, targets, tiles, *arrays, *extras)


def shards(
    features,
    cotangent,
    w_self,
    w_neigh,
    bias_term,
    block_tiles,
    block_rows,
    block_cols,
    block_counts,
):
    tiles, rows, cols = block_tiles[0, 0], block_rows[0, 0], block_cols[0, 0]
    live = jnp.arange(SLOTS) < block_counts[0, 0]
    x, zl, core = coordinate("x"), coordinate("zl"), coordinate("core")
    zh, y = coordinate("zh"), coordinate("y")
    place = 2 * ((cols // 16 - x) % 4) + (cols // 8 - zl) % 2
    col_ids = (look_up(PLANE_PLACE, place) + 8 * ((cols // 4 - core) % 2)) * 4 + cols % 4
    place = 4 * look_up(RING_PLACE, (rows // 16 - zh) % 4)
    row_ids = (place + look_up(RING_PLACE, (rows // 4 - y) % 4)) * 4 + rows % 4
    row_targets = jnp.where(live, row_ids, BLOCKS)
    col_targets = jnp.where(live, col_ids, BLOCKS)


    sums = degrees(row_targets, tiles)
    extra = jnp.pad(sums.reshape(16, 2, F), ((0, 0), (0, 14), (0, 0))).astype(bf16)
    pieces, place = [], 0
    for chunk in gather_row(features, sums):
        pieces.append((chunk, 0, chunk.shape[0], place))
        place += chunk.shape[0]
    whole = scatter_col(products(False, col_ids, row_targets, pieces, COL_PARTS, tiles, extra))
    aggregate, degree = whole[:CHUNK], whole[CHUNK : CHUNK + 2].reshape(CHUNK)

    scale = lax.rsqrt(1.0 + degree)
    neigh = (scale[:, None] * aggregate).astype(bf16)
    pre = (
        jnp.dot(features, w_self, preferred_element_type=f32)
        + jnp.dot(neigh, w_neigh, preferred_element_type=f32)
        + bias_term.astype(f32)
    )
    sigma = jax.nn.sigmoid(pre)
    activation = (pre * sigma).astype(bf16)
    dpre = (cotangent.astype(f32) * sigma * (1.0 + pre * (1.0 - sigma))).astype(bf16)
    contract_cols = (((1,), (1,)), ((), ()))
    back = (
        scale[:, None] * lax.dot_general(dpre, w_neigh, contract_cols, preferred_element_type=f32)
    ).astype(bf16)

    def local_grads(features, neigh, dpre):
        contract_rows = (((0,), (0,)), ((), ()))
        local_self = lax.dot_general(features, dpre, contract_rows, preferred_element_type=f32)
        local_neigh = lax.dot_general(neigh, dpre, contract_rows, preferred_element_type=f32)
        local_bias = jnp.sum(dpre.astype(f32), axis=0)
        local_bias = jnp.pad(local_bias[None], ((0, 31), (0, 0)))
        return jnp.concatenate([local_self, local_neigh, local_bias], 0)

    grads = Sums(local_grads, features, neigh, dpre)
    pieces = gather_col(back, grads)
    partial_src = products(True, row_ids, col_targets, pieces, ROW_PARTS, tiles)
    own_term = lax.dot_general(dpre, w_self, contract_cols, preferred_element_type=f32)
    grad_features = (own_term + scatter_row(partial_src, grads)).astype(bf16)
    grads.step()
    grads = grads.now * (1.0 / jnp.sqrt(f32(CHUNK * 256)))
    return activation, grad_features, grads[:F], grads[F : 2 * F], grads[2 * F]


def solution(mesh):
    return jax.shard_map(
        shards,
        mesh=mesh,
        in_specs=(
            P(("row", "col"), None),
            P(("row", "col"), None),
            P(),
            P(),
            P(),
            P("row", "col", None, None, None),
            P("row", "col", None),
            P("row", "col", None),
            P("row", "col"),
        ),
        out_specs=(P(("row", "col"), None), P(("row", "col"), None), P(), P(), P()),
        check_vma=False,
    )
```
